32 devices in a mesh: grp: 8 (over y, x, core), qtr: 4 (over z).
Axes of the slice: x: 2, y: 2, z: 4, core: 2. Of those that a mesh axis runs over, the one named last changes fastest.
Arguments:
- vectors: float32 [8192, 512], P(('grp', 'qtr')), may hold values from -6 to 6
- previous: float32 [8192, 512], P(('grp', 'qtr')), may hold values from -6 to 6
- diag_tiles: bfloat16 [64, 4, 128, 128], P(('grp', 'qtr')), may hold values from -0.125 to 0.125
- diag_cols: int32 [64, 4], P(('grp', 'qtr')), may hold values from 0 to 7, all different within a row
- diag_mask: int32 [64, 4], P(('grp', 'qtr')), may hold values 0 or 1
- off_tiles: bfloat16 [3, 64, 4, 128, 128], P(None, ('grp', 'qtr')), may hold values from -0.125 to 0.125
- off_rows: int32 [3, 64, 4], P(None, ('grp', 'qtr')), may hold values from 0 to 7, all different within a row
- off_mask: int32 [3, 64, 4], P(None, ('grp', 'qtr')), may hold values 0 or 1
Outputs:
- chebyshev: float32 [8192, 512], P(('grp', 'qtr'))
The draws below stay inside these ranges and needn't reach their ends.
Inputs may be any that keep to these rules, and one draw needn't show every extreme that they name: `diag_cols`: each row names 4 different tile columns of the group. `off_rows`: each row names 4 different tile rows of the group.
All inputs are finite; a program needn't handle non-finite values. No bound on the sum of `diag_mask` or of `off_mask` on one device may be relied on, other than what follows from the above.
Results may differ from the reference program's by a relative error of at most 0.002.
Values may be sent and summed in bfloat16 or wider, within the bound.
A program may use at most 64 MiB of HBM per device.

```python
import jax
import jax.numpy as jnp
from jax import lax

K = 512
TILE = 128
TR_DEV = 2
GROUP_TILES = 8
SLOTS = 4
ROWS = 8192
N_GRP = 8
N_QTR = 4


def with_ends(drawn, stream_key, least, high):
    spot = [jax.random.randint(jax.random.fold_in(stream_key, axis), (), 0, length) for axis, length in enumerate(drawn.shape)]
    widest = drawn.shape.index(max(drawn.shape))
    next_to = spot[:widest] + [(spot[widest] + 1) % drawn.shape[widest]] + spot[widest + 1:]
    return drawn.at[tuple(spot)].set(least).at[tuple(next_to)].set(high)


def level_of(rng, shape, split, least, largest):
    factor_of = 1.0
    for dim, blocks in split:
        steps = jax.random.uniform(jax.random.fold_in(jax.random.fold_in(rng, 6), dim), (blocks,), jnp.float32, least / len(split), largest / len(split))
        factor_of = factor_of * jnp.repeat(jnp.exp(steps), shape[dim] // blocks).reshape((-1,) + (1,) * (len(shape) - 1 - dim))
    return factor_of


def different_ones(rng, rows, amount, top, lift):
    ranking = jax.random.permutation(jax.random.fold_in(rng, 1), amount)
    favour = ranking
    for power in range(3):
        favour = favour * favour // amount
    favour = favour * lift // amount
    tickets = jax.random.randint(jax.random.fold_in(rng, 2), (rows, amount), 0, 4096) + favour
    holders = jax.random.permutation(jax.random.fold_in(rng, 3), rows)[jnp.arange(amount) % rows]
    tickets = jnp.where(jnp.arange(rows)[:, None] == holders[None, :], 1 << 14, tickets)
    priority = tickets * amount + jnp.arange(amount)
    return lax.top_k(priority.astype(jnp.int32), top)[1].astype(jnp.int32)


def bell_draw(own_key, dims, deviation, limit, shards=(), kind=jnp.bfloat16):
    drawn = jax.random.normal(own_key, dims, jnp.float32) * deviation
    if len(shards) > 0:
        drawn = level_of(own_key, dims, shards, -0.22, 0.18) * drawn
    return jnp.clip(drawn, min=-limit, max=limit).astype(kind)


def setup_inputs(seed: int = 0) -> dict:
    seeds = jax.random.split(jax.random.key(seed), 9)
    vectors = bell_draw(seeds[0], (ROWS, K), 1.0, 6.0, ((0, 32),), jnp.float32)
    previous = bell_draw(seeds[1], (ROWS, K), 1.0, 6.0, ((0, 32),), jnp.float32)
    diag_tiles = bell_draw(seeds[2], (N_GRP * GROUP_TILES, SLOTS, TILE, TILE), (4 * SLOTS * TILE) ** -0.5, 0.125, ((0, 32),))
    diag_cols = different_ones(seeds[3], (N_GRP * GROUP_TILES), GROUP_TILES, SLOTS, 0)
    diag_mask = with_ends((jax.random.randint(seeds[4], (N_GRP * GROUP_TILES, SLOTS), 0, 2) < 1).astype(jnp.int32), jax.random.fold_in(seeds[4], 1), 0, 1)
    off_tiles = bell_draw(seeds[5], (3, N_GRP * GROUP_TILES, SLOTS, TILE, TILE), (4 * SLOTS * TILE) ** -0.5, 0.125, ((1, 32),))
    off_rows = different_ones(seeds[6], 3 * (N_GRP * GROUP_TILES), GROUP_TILES, SLOTS, 0).reshape((3, N_GRP * GROUP_TILES, SLOTS))
    off_mask = with_ends((jax.random.randint(seeds[7], (3, N_GRP * GROUP_TILES, SLOTS), 0, 2) < 1).astype(jnp.int32), jax.random.fold_in(seeds[7], 1), 0, 1)
    return dict(vectors=vectors, previous=previous, diag_tiles=diag_tiles, diag_cols=diag_cols, diag_mask=diag_mask, off_tiles=off_tiles, off_rows=off_rows, off_mask=off_mask)


cheb_center = 0.25
cheb_half = 2.0


def reference(vectors, previous, diag_tiles, diag_cols, diag_mask, off_tiles, off_rows, off_mask):
    group_tiles = TR_DEV * N_QTR
    levels = N_GRP.bit_length() - 1
    bit_list = [0, levels // 2, levels - 1]
    rounded = lax.optimization_barrier(vectors.astype(jnp.bfloat16))
    vec_full = rounded.astype(jnp.float32).reshape(N_GRP, group_tiles, TILE, K)
    diag_shaped = diag_tiles.reshape(N_GRP, group_tiles, SLOTS, TILE, TILE)
    diag_flags = diag_mask.reshape(N_GRP, group_tiles, SLOTS)
    diag_index = diag_cols.reshape(N_GRP, group_tiles, SLOTS).astype(jnp.int32)
    off_shaped = off_tiles.reshape(3, N_GRP, group_tiles, SLOTS, TILE, TILE)
    off_flags = off_mask.reshape(3, N_GRP, group_tiles, SLOTS)
    off_index = off_rows.reshape(3, N_GRP, group_tiles, SLOTS).astype(jnp.int32)
    highest = lax.Precision.HIGHEST

    def live_tiles(tile_set, flags):
        return tile_set.astype(jnp.float32) * flags[..., None, None].astype(jnp.float32)

    def one_group(index):
        own_vecs = vec_full[index]
        tile_set = live_tiles(diag_shaped[index], diag_flags[index])
        col_set = diag_index[index]
        result = jnp.einsum('tsab,tsbk->tak', tile_set, own_vecs[col_set], precision=highest)
        result = result.at[col_set].add(jnp.einsum('tsab,tak->tsbk', tile_set, own_vecs, precision=highest))
        for partner in range(3):
            other = jnp.bitwise_xor(index, jnp.int32(1 << bit_list[partner])).astype(jnp.int32)
            other_vecs = vec_full[other]
            mine = live_tiles(off_shaped[partner, index], off_flags[partner, index])
            mine_rows = off_index[partner, index]
            result = result.at[mine_rows].add(jnp.einsum('csab,cbk->csak', mine, other_vecs, precision=highest))
            theirs = live_tiles(off_shaped[partner, other], off_flags[partner, other])
            their_rows = off_index[partner, other]
            result = result + jnp.einsum('csab,csak->cbk', theirs, other_vecs[their_rows], precision=highest)
        return result

    applied = lax.map(one_group, jnp.arange(N_GRP, dtype=jnp.int32)).reshape(N_GRP * group_tiles * TILE, K)
    return (2.0 / cheb_half) * (applied - cheb_center * vectors) - previous
```

```python
import functools

import jax
import jax.numpy as jnp
from jax import lax
from jax.experimental import pallas as pl
from jax.experimental.pallas import tpu as pltpu
from jax.sharding import PartitionSpec as P

cheb_center = 0.25
cheb_half = 2.0
partners = 3
chunks = 2
MESH = pl.DeviceIdType.MESH
f32 = jnp.float32
bf16 = jnp.bfloat16


def flip(index, bit):
    step = 1 << bit
    return index + step - 2 * step * ((index // step) % 2)


def dot(left, right):
    return jnp.dot(left, right, preferred_element_type=f32)


def kernel(
    quarters, bit_list,
    dcols, dmask, orows, omask, vec_hbm, prev_hbm, diag_hbm, off_hbm,
    out,
    vec, prev, diag, off, tiles, tiles_t, w, wt, own, pvec, prod_out, prod_in,
    inbox, outbox, acc, terms,
    load_sem, z_send, z_recv, p_send, p_recv,
):
    Q = quarters
    g = lax.axis_index("grp")
    q = lax.axis_index("qtr")
    rows = own.shape[1]
    width = own.shape[2]
    tile = tiles.shape[-1]
    strips = rows // tile
    slots = diag.shape[1]
    has_left = q > 0
    has_right = q < Q - 1
    back = Q - 1 - q
    peers = [(flip(g, bit), q) for bit in bit_list]
    sides = ((g, q - 1), (g, q + 1))
    has_side = (has_left, has_right)

    loads = [
        pltpu.make_async_copy(src, dst, load_sem.at[i])
        for i, (src, dst) in enumerate(
            ((vec_hbm, vec), (diag_hbm, diag), (off_hbm, off), (prev_hbm, prev))
        )
    ]
    for load in loads:
        load.start()

    barrier = pltpu.get_barrier_semaphore()
    for peer in peers:
        pl.semaphore_signal(barrier, inc=1, device_id=peer, device_id_type=MESH)
    for side in range(2):
        @pl.when(has_side[side])
        def _():
            pl.semaphore_signal(barrier, inc=1, device_id=sides[side], device_id_type=MESH)

    loads[0].wait()
    for c in range(chunks):
        own[c] = vec[:, c * width:(c + 1) * width].astype(bf16)

    neighbours = jnp.where(has_left, 1, 0) + jnp.where(has_right, 1, 0)
    pl.semaphore_wait(barrier, partners + neighbours)

    def z_copy(src, to_right, idx, c):
        lane = 0 if to_right else 1
        return pltpu.make_async_remote_copy(
            src_ref=src,
            dst_ref=inbox.at[lane, idx, c],
            send_sem=z_send.at[lane, idx, c],
            recv_sem=z_recv.at[lane, idx, c],
            device_id=sides[1 if to_right else 0],
            device_id_type=MESH,
        )

    def p_copy(kind, j, c):
        return pltpu.make_async_remote_copy(
            src_ref=own.at[c] if kind == 0 else prod_out.at[j, c],
            dst_ref=pvec.at[j, c] if kind == 0 else prod_in.at[j, c],
            send_sem=p_send.at[kind, j, c],
            recv_sem=p_recv.at[kind, j, c],
            device_id=peers[j],
            device_id_type=MESH,
        )

    for c in range(chunks):
        @pl.when(has_right)
        def _():
            z_copy(own.at[c], True, 0, c).start()

        @pl.when(has_left)
        def _():
            z_copy(own.at[c], False, 0, c).start()

        for j in reversed(range(partners)):
            p_copy(0, j, c).start()

    loads[1].wait()
    loads[2].wait()
    zero = jnp.zeros((tile, tile), bf16)
    blocks = strips * (1 + partners)
    for n in range(blocks):
        tiles[n, 0] = zero
        tiles_t[n, 0] = zero
        for s in range(slots):
            if n < strips:
                block = diag[n, s]
                tiles[n, s + 1] = block.T
                tiles_t[n, s + 1] = block
            else:
                block = off[n // strips - 1, n % strips, s]
                tiles[n, s + 1] = block
                tiles_t[n, s + 1] = block.T
    for n in range(blocks):
        if n < strips:
            targets = [dcols[n, s] for s in range(slots)]
            flags = [dmask[n, s] * (s + 1) for s in range(slots)]
        else:
            j, k = n // strips - 1, n % strips
            targets = [orows[j, k, s] for s in range(slots)]
            flags = [omask[j, k, s] * (s + 1) for s in range(slots)]
        for r in range(strips * Q):
            place = jnp.int32(0)
            for s in range(slots):
                place = place + jnp.where(targets[s] == r, flags[s], 0)
            d, k = r // strips, r % strips
            w[d, k * tile:(k + 1) * tile, n * tile:(n + 1) * tile] = tiles[n, place]
            wt[d, n * tile:(n + 1) * tile, k * tile:(k + 1) * tile] = tiles_t[n, place]

    def gather_step(idx, c):
        for side, count, src in ((0, q, q - 1 - idx), (1, back, q + 1 + idx)):
            @pl.when(idx < count)
            def _():
                acc[c] += dot(wt[src], inbox[side, idx, c])

    for idx in range(Q):
        for c in range(chunks):
            for side, count in ((0, q), (1, back)):
                to_right = side == 0

                @pl.when(has_side[side])
                def _():
                    z_copy(outbox.at[side, idx, c], to_right, idx, c).wait_recv()

                if idx < Q - 1:
                    @pl.when((idx < count) & has_side[1 - side])
                    def _():
                        z_copy(inbox.at[side, idx, c], to_right, idx + 1, c).start()

            if idx == 0:
                for j in range(partners):
                    p_copy(0, j, c).wait_recv()
                for d in range(Q):
                    total = dot(w[d, :, :rows], own[c])
                    for j in range(partners):
                        total += dot(w[d, :, (j + 1) * rows:(j + 2) * rows], pvec[j, c])
                    terms[d, c] = total

            if idx < Q - 1:
                for side, count in ((0, q), (1, back)):
                    to_right = side == 0
                    dest = Q - 1 - idx + q if to_right else idx - back

                    @pl.when((idx >= count) & has_side[1 - side] & has_side[side])
                    def _():
                        outbox[side, idx + 1, c] = (
                            terms[dest, c] + inbox[side, idx, c].astype(f32)
                        ).astype(bf16)

                    @pl.when((idx >= count) & has_side[1 - side] & (count == 0))
                    def _():
                        outbox[side, idx + 1, c] = terms[dest, c].astype(bf16)

                    @pl.when((idx >= count) & has_side[1 - side])
                    def _():
                        z_copy(outbox.at[side, idx + 1, c], to_right, idx + 1, c).start()

            if idx == 0:
                acc[c] = dot(wt[q], own[c])
            if idx < Q - 1:
                gather_step(idx, c)
                last = jnp.maximum(q, back) - 1

                @pl.when(idx == last)
                def _():
                    for j in reversed(range(partners)):
                        prod_out[j, c] = acc[c, (j + 1) * rows:(j + 2) * rows].astype(bf16)
                        p_copy(1, j, c).start()

            if idx == Q - 1:
                if c == 0:
                    loads[3].wait()
                total = acc[c, :rows] + terms[q, c]
                for j in range(partners):
                    p_copy(1, j, c).wait_recv()
                    total += prod_in[j, c].astype(f32)
                acc[c, :rows] = total
                for side in range(2):
                    @pl.when(has_side[side])
                    def _():
                        acc[c, :rows] += inbox[side, idx, c].astype(f32)
                cols = slice(c * width, (c + 1) * width)
                out[:, cols] = (
                    2.0 / cheb_half * (acc[c, :rows] - cheb_center * vec[:, cols]) - prev[:, cols]
                )

    for c in range(chunks):
        for kind in range(2):
            for j in range(partners):
                p_copy(kind, j, c).wait_send()
        for idx in range(Q):
            for side in range(2):
                @pl.when(has_side[1 - side])
                def _():
                    z_copy(outbox.at[side, idx, c], side == 0, idx, c).wait_send()


def on_device(vectors, previous, diag_tiles, diag_cols, diag_mask, off_tiles, off_rows, off_mask):
    tile = diag_tiles.shape[-1]
    strips, slots = diag_tiles.shape[:2]
    rows, vec_width = vectors.shape
    quarters = lax.axis_size("qtr")
    levels = lax.axis_size("grp").bit_length() - 1
    bit_list = (0, levels // 2, levels - 1)
    width = vec_width // chunks
    blocks = strips * (1 + partners)
    whole = blocks * tile
    smem = pl.BlockSpec(memory_space=pltpu.SMEM)
    hbm = pl.BlockSpec(memory_space=pl.ANY)
    dma = pltpu.SemaphoreType.DMA
    macs = 2 * whole * quarters * rows * vec_width
    return pl.pallas_call(
        functools.partial(kernel, quarters, bit_list),
        out_shape=jax.ShapeDtypeStruct((rows, vec_width), f32),
        in_specs=[smem] * 4 + [hbm] * 4,
        out_specs=pl.BlockSpec(memory_space=pltpu.VMEM),
        scratch_shapes=[
            pltpu.VMEM((rows, vec_width), f32),
            pltpu.VMEM((rows, vec_width), f32),
            pltpu.VMEM(diag_tiles.shape, bf16),
            pltpu.VMEM(off_tiles.shape, bf16),
            pltpu.VMEM((blocks, slots + 1, tile, tile), bf16),
            pltpu.VMEM((blocks, slots + 1, tile, tile), bf16),
            pltpu.VMEM((quarters, rows, whole), bf16),
            pltpu.VMEM((quarters, whole, rows), bf16),
            pltpu.VMEM((chunks, rows, width), bf16),
            pltpu.VMEM((partners, chunks, rows, width), bf16),
            pltpu.VMEM((partners, chunks, rows, width), bf16),
            pltpu.VMEM((partners, chunks, rows, width), bf16),
            pltpu.VMEM((2, quarters, chunks, rows, width), bf16),
            pltpu.VMEM((2, quarters, chunks, rows, width), bf16),
            pltpu.VMEM((chunks, whole, width), f32),
            pltpu.VMEM((quarters, chunks, rows, width), f32),
            dma((4,)),
            dma((2, quarters, chunks)),
            dma((2, quarters, chunks)),
            dma((2, partners, chunks)),
            dma((2, partners, chunks)),
        ],
        compiler_params=pltpu.CompilerParams(
            collective_id=0, has_side_effects=True, vmem_limit_bytes=48 << 20
        ),
        cost_estimate=pl.CostEstimate(
            flops=2 * macs, bytes_accessed=4 * rows * vec_width * 4, transcendentals=0
        ),
    )(diag_cols, diag_mask, off_rows, off_mask, vectors, previous, diag_tiles, off_tiles)


def solution(mesh):
    in_specs = (
        P(("grp", "qtr"), None),
        P(("grp", "qtr"), None),
        P(("grp", "qtr"), None, None, None),
        P(("grp", "qtr"), None),
        P(("grp", "qtr"), None),
        P(None, ("grp", "qtr"), None, None, None),
        P(None, ("grp", "qtr"), None),
        P(None, ("grp", "qtr"), None),
    )
    out_specs = P(("grp", "qtr"), None)
    return jax.shard_map(
        on_device, mesh=mesh, in_specs=in_specs, out_specs=out_specs, check_vma=False
    )
```

```python
import functools

import jax
import jax.numpy as jnp
from jax import lax
from jax.experimental import pallas as pl
from jax.experimental.pallas import tpu as pltpu
from jax.sharding import PartitionSpec as P

cheb_center = 0.25
cheb_half = 2.0
partners = 3
chunks = 2
MESH = pl.DeviceIdType.MESH
f32 = jnp.float32
bf16 = jnp.bfloat16


def flip(index, bit):
    step = 1 << bit
    return index + step - 2 * step * ((index // step) % 2)


def dot(left, right):
    return jnp.dot(left, right, preferred_element_type=f32)


def kernel(
    quarters, bit_list,
    dcols_hbm, dmask_hbm, orows_hbm, omask_hbm, vec_hbm, prev_hbm, diag_hbm, off_hbm,
    out,
    dcols, dmask, orows, omask, vec, prev, diag, off, tiles, tiles_t, w, wt, own, pvec, prod_out, prod_in,
    inbox, outbox, acc, terms,
    load_sem, z_send, z_recv, p_send, p_recv,
):
    Q = quarters
    g = lax.axis_index("grp")
    q = lax.axis_index("qtr")
    rows = own.shape[1]
    width = own.shape[2]
    tile = tiles.shape[-1]
    strips = rows // tile
    slots = diag.shape[1]
    has_left = q > 0
    has_right = q < Q - 1
    back = Q - 1 - q
    peers = [(flip(g, bit), q) for bit in bit_list]
    sides = ((g, q - 1), (g, q + 1))
    has_side = (has_left, has_right)

    loads = [
        pltpu.make_async_copy(src, dst, load_sem.at[i])
        for i, (src, dst) in enumerate(
            (
                (vec_hbm, vec), (dcols_hbm, dcols), (dmask_hbm, dmask), (orows_hbm, orows),
                (omask_hbm, omask), (diag_hbm, diag), (off_hbm, off), (prev_hbm, prev),
            )
        )
    ]
    for load in loads:
        load.start()

    barrier = pltpu.get_barrier_semaphore()
    for peer in peers:
        pl.semaphore_signal(barrier, inc=1, device_id=peer, device_id_type=MESH)
    for side in range(2):
        @pl.when(has_side[side])
        def _():
            pl.semaphore_signal(barrier, inc=1, device_id=sides[side], device_id_type=MESH)

    loads[0].wait()
    for c in range(chunks):
        own[c] = vec[:, c * width:(c + 1) * width].astype(bf16)

    neighbours = jnp.where(has_left, 1, 0) + jnp.where(has_right, 1, 0)
    pl.semaphore_wait(barrier, partners + neighbours)

    def z_copy(src, to_right, idx, c, h):
        lane = 0 if to_right else 1
        part = pl.ds(h * tile, tile)
        return pltpu.make_async_remote_copy(
            src_ref=src.at[part],
            dst_ref=inbox.at[lane, idx, c, part],
            send_sem=z_send.at[lane, idx, c, h],
            recv_sem=z_recv.at[lane, idx, c, h],
            device_id=sides[1 if to_right else 0],
            device_id_type=MESH,
        )

    def p_copy(kind, j, c):
        return pltpu.make_async_remote_copy(
            src_ref=own.at[c] if kind == 0 else prod_out.at[j, c],
            dst_ref=pvec.at[j, c] if kind == 0 else prod_in.at[j, c],
            send_sem=p_send.at[kind, j, c],
            recv_sem=p_recv.at[kind, j, c],
            device_id=peers[j],
            device_id_type=MESH,
        )

    for c in range(chunks):
        for h in range(strips):
            @pl.when(has_right)
            def _():
                z_copy(own.at[c], True, 0, c, h).start()

            @pl.when(has_left)
            def _():
                z_copy(own.at[c], False, 0, c, h).start()

        for j in reversed(range(partners)):
            p_copy(0, j, c).start()

    for load in loads[1:7]:
        load.wait()
    zero = jnp.zeros((tile, tile), bf16)
    blocks = strips * (1 + partners)

    def block_of(n, s):
        return diag[n, s] if n < strips else off[n // strips - 1, n % strips, s]

    def places(n):
        if n < strips:
            targets = [dcols[n, s] for s in range(slots)]
            flags = [dmask[n, s] * (s + 1) for s in range(slots)]
        else:
            j, k = n // strips - 1, n % strips
            targets = [orows[j, k, s] for s in range(slots)]
            flags = [omask[j, k, s] * (s + 1) for s in range(slots)]
        for r in range(strips * Q):
            place = jnp.int32(0)
            for s in range(slots):
                place = place + jnp.where(targets[s] == r, flags[s], 0)
            yield r // strips, (r % strips) * tile, place

    def fill(held, across, put):
        for n in range(blocks):
            held[n, 0] = zero
            for s in range(slots):
                block = block_of(n, s)
                held[n, s + 1] = block.T if (n < strips) == across else block
        for n in range(blocks):
            for d, low, place in places(n):
                put(d, low, n * tile, held[n, place])

    def put_w(d, low, col, block):
        w[d, low:low + tile, col:col + tile] = block

    def put_wt(d, low, col, block):
        wt[d, col:col + tile, low:low + tile] = block

    fill(tiles, True, put_w)

    def gather_step(idx, c):
        for side, count, src in ((0, q, q - 1 - idx), (1, back, q + 1 + idx)):
            @pl.when(idx < count)
            def _():
                acc[c] += dot(wt[src], inbox[side, idx, c])

    def arrive(idx, c, h):
        for side, count in ((0, q), (1, back)):
            to_right = side == 0

            @pl.when(has_side[side])
            def _():
                z_copy(outbox.at[side, idx, c], to_right, idx, c, h).wait_recv()

            if idx < Q - 1:
                @pl.when((idx < count) & has_side[1 - side])
                def _():
                    z_copy(inbox.at[side, idx, c], to_right, idx + 1, c, h).start()

    def reduce_on(idx, c, h):
        part = slice(h * tile, (h + 1) * tile)
        for side, count in ((0, q), (1, back)):
            to_right = side == 0
            dest = Q - 1 - idx + q if to_right else idx - back
            goes = (idx >= count) & has_side[1 - side]

            @pl.when(goes & has_side[side])
            def _():
                outbox[side, idx + 1, c, part] = (
                    terms[dest, c, part] + inbox[side, idx, c, part].astype(f32)
                ).astype(bf16)

            @pl.when(goes & (count == 0))
            def _():
                outbox[side, idx + 1, c, part] = terms[dest, c, part].astype(bf16)

            @pl.when(goes)
            def _():
                z_copy(outbox.at[side, idx + 1, c], to_right, idx + 1, c, h).start()

    for c in range(chunks):
        for h in range(strips):
            arrive(0, c, h)
        for j in range(partners):
            p_copy(0, j, c).wait_recv()
        for d in range(Q):
            total = dot(w[d, :, :rows], own[c])
            for j in range(partners):
                total += dot(w[d, :, (j + 1) * rows:(j + 2) * rows], pvec[j, c])
            terms[d, c] = total
        for h in range(strips):
            reduce_on(0, c, h)

    fill(tiles_t, False, put_wt)

    for idx in range(1, Q - 1):
        for c in range(chunks):
            for h in range(strips):
                arrive(idx, c, h)
                reduce_on(idx, c, h)
            if idx == 1:
                acc[c] = dot(wt[q], own[c])
                gather_step(0, c)
            gather_step(idx, c)
            last = jnp.maximum(jnp.maximum(q, back) - 1, 1)

            @pl.when(idx == last)
            def _():
                for j in reversed(range(partners)):
                    prod_out[j, c] = acc[c, (j + 1) * rows:(j + 2) * rows].astype(bf16)
                    p_copy(1, j, c).start()

    loads[7].wait()
    for c in range(chunks):
        cols = slice(c * width, (c + 1) * width)
        total = acc[c, :rows] + terms[q, c]
        for j in range(partners):
            p_copy(1, j, c).wait_recv()
            total += prod_in[j, c].astype(f32)
        out[:, cols] = 2.0 / cheb_half * (total - cheb_center * vec[:, cols]) - prev[:, cols]
        for h in range(strips):
            part = slice(h * tile, (h + 1) * tile)
            arrive(Q - 1, c, h)
            for side in range(2):
                @pl.when(has_side[side])
                def _():
                    out[part, cols] += 2.0 / cheb_half * inbox[side, Q - 1, c, part].astype(f32)

    for c in range(chunks):
        for kind in range(2):
            for j in range(partners):
                p_copy(kind, j, c).wait_send()
        for idx in range(Q):
            for h in range(strips):
                for side in range(2):
                    @pl.when(has_side[1 - side])
                    def _():
                        z_copy(outbox.at[side, idx, c], side == 0, idx, c, h).wait_send()


def on_device(vectors, previous, diag_tiles, diag_cols, diag_mask, off_tiles, off_rows, off_mask):
    tile = diag_tiles.shape[-1]
    strips, slots = diag_tiles.shape[:2]
    rows, vec_width = vectors.shape
    quarters = lax.axis_size("qtr")
    levels = lax.axis_size("grp").bit_length() - 1
    bit_list = (0, levels // 2, levels - 1)
    width = vec_width // chunks
    blocks = strips * (1 + partners)
    whole = blocks * tile
    hbm = pl.BlockSpec(memory_space=pltpu.HBM)
    dma = pltpu.SemaphoreType.DMA
    macs = 2 * whole * quarters * rows * vec_width
    return pl.pallas_call(
        functools.partial(kernel, quarters, bit_list),
        out_shape=jax.ShapeDtypeStruct((rows, vec_width), f32),
        in_specs=[hbm] * 8,
        out_specs=pl.BlockSpec(memory_space=pltpu.VMEM),
        scratch_shapes=[
            pltpu.SMEM(diag_cols.shape, jnp.int32),
            pltpu.SMEM(diag_mask.shape, jnp.int32),
            pltpu.SMEM(off_rows.shape, jnp.int32),
            pltpu.SMEM(off_mask.shape, jnp.int32),
            pltpu.VMEM((rows, vec_width), f32),
            pltpu.VMEM((rows, vec_width), f32),
            pltpu.VMEM(diag_tiles.shape, bf16),
            pltpu.VMEM(off_tiles.shape, bf16),
            pltpu.VMEM((blocks, slots + 1, tile, tile), bf16),
            pltpu.VMEM((blocks, slots + 1, tile, tile), bf16),
            pltpu.VMEM((quarters, rows, whole), bf16),
            pltpu.VMEM((quarters, whole, rows), bf16),
            pltpu.VMEM((chunks, rows, width), bf16),
            pltpu.VMEM((partners, chunks, rows, width), bf16),
            pltpu.VMEM((partners, chunks, rows, width), bf16),
            pltpu.VMEM((partners, chunks, rows, width), bf16),
            pltpu.VMEM((2, quarters, chunks, rows, width), bf16),
            pltpu.VMEM((2, quarters, chunks, rows, width), bf16),
            pltpu.VMEM((chunks, whole, width), f32),
            pltpu.VMEM((quarters, chunks, rows, width), f32),
            dma((8,)),
            dma((2, quarters, chunks, strips)),
            dma((2, quarters, chunks, strips)),
            dma((2, partners, chunks)),
            dma((2, partners, chunks)),
        ],
        compiler_params=pltpu.CompilerParams(
            collective_id=0, has_side_effects=True, vmem_limit_bytes=64 << 20
        ),
        cost_estimate=pl.CostEstimate(
            flops=2 * macs, bytes_accessed=4 * rows * vec_width * 4, transcendentals=0
        ),
    )(diag_cols, diag_mask, off_rows, off_mask, vectors, previous, diag_tiles, off_tiles)


def solution(mesh):
    in_specs = (
        P(("grp", "qtr"), None),
        P(("grp", "qtr"), None),
        P(("grp", "qtr"), None, None, None),
        P(("grp", "qtr"), None),
        P(("grp", "qtr"), None),
        P(None, ("grp", "qtr"), None, None, None),
        P(None, ("grp", "qtr"), None),
        P(None, ("grp", "qtr"), None),
    )
    out_specs = P(("grp", "qtr"), None)
    return jax.shard_map(
        on_device, mesh=mesh, in_specs=in_specs, out_specs=out_specs, check_vma=False
    )
```

```python
import functools

import jax
import jax.numpy as jnp
from jax import lax
from jax.experimental import pallas as pl
from jax.experimental.pallas import tpu as pltpu
from jax.sharding import PartitionSpec as P

cheb_center = 0.25
cheb_half = 2.0
partners = 3
chunks = 2
MESH = pl.DeviceIdType.MESH
f32 = jnp.float32
bf16 = jnp.bfloat16


def flip(index, bit):
    step = 1 << bit
    return index + step - 2 * step * ((index // step) % 2)


def dot(left, right):
    return jnp.dot(left, right, preferred_element_type=f32)


def kernel(
    quarters, bit_list,
    dcols_hbm, dmask_hbm, orows_hbm, omask_hbm, vec_hbm, prev_hbm, diag_hbm, off_hbm,
    out,
    dcols, dmask, orows, omask, vec, prev, diag, off, tiles, tiles_t, w, wt, own, pvec, prod_out, prod_in,
    inbox, outbox, acc, terms,
    load_sem, z_send, z_recv, p_send, p_recv,
):
    Q = quarters
    g = lax.axis_index("grp")
    q = lax.axis_index("qtr")
    rows = own.shape[1]
    width = own.shape[2]
    tile = tiles.shape[-1]
    strips = rows // tile
    slots = diag.shape[1]
    has_left = q > 0
    has_right = q < Q - 1
    back = Q - 1 - q
    peers = [(flip(g, bit), q) for bit in bit_list]
    sides = ((g, q - 1), (g, q + 1))
    has_side = (has_left, has_right)

    loads = [
        pltpu.make_async_copy(src, dst, load_sem.at[i])
        for i, (src, dst) in enumerate(
            (
                (vec_hbm, vec), (dcols_hbm, dcols), (dmask_hbm, dmask), (orows_hbm, orows),
                (omask_hbm, omask), (diag_hbm, diag), (off_hbm, off), (prev_hbm, prev),
            )
        )
    ]
    for load in loads:
        load.start()

    barrier = pltpu.get_barrier_semaphore()
    for peer in peers:
        pl.semaphore_signal(barrier, inc=1, device_id=peer, device_id_type=MESH)
    for side in range(2):
        @pl.when(has_side[side])
        def _():
            pl.semaphore_signal(barrier, inc=1, device_id=sides[side], device_id_type=MESH)

    loads[0].wait()
    for c in range(chunks):
        own[c] = vec[:, c * width:(c + 1) * width].astype(bf16)

    neighbours = jnp.where(has_left, 1, 0) + jnp.where(has_right, 1, 0)
    pl.semaphore_wait(barrier, partners + neighbours)

    def z_copy(src, to_right, idx, c, h):
        lane = 0 if to_right else 1
        part = pl.ds(h * tile, tile)
        return pltpu.make_async_remote_copy(
            src_ref=src.at[part],
            dst_ref=inbox.at[lane, idx, c, part],
            send_sem=z_send.at[lane, idx, c, h],
            recv_sem=z_recv.at[lane, idx, c, h],
            device_id=sides[1 if to_right else 0],
            device_id_type=MESH,
        )

    def p_copy(kind, j, c):
        return pltpu.make_async_remote_copy(
            src_ref=own.at[c] if kind == 0 else prod_out.at[j, c],
            dst_ref=pvec.at[j, c] if kind == 0 else prod_in.at[j, c],
            send_sem=p_send.at[kind, j, c],
            recv_sem=p_recv.at[kind, j, c],
            device_id=peers[j],
            device_id_type=MESH,
        )

    def send_own(c):
        for h in range(strips):
            @pl.when(has_right)
            def _():
                z_copy(own.at[c], True, 0, c, h).start()

            @pl.when(has_left)
            def _():
                z_copy(own.at[c], False, 0, c, h).start()

        for j in reversed(range(partners)):
            p_copy(0, j, c).start()

    send_own(0)

    for load in loads[1:7]:
        load.wait()
    zero = jnp.zeros((tile, tile), bf16)
    blocks = strips * (1 + partners)

    def block_of(n, s):
        return diag[n, s] if n < strips else off[n // strips - 1, n % strips, s]

    def places(n):
        if n < strips:
            targets = [dcols[n, s] for s in range(slots)]
            flags = [dmask[n, s] * (s + 1) for s in range(slots)]
        else:
            j, k = n // strips - 1, n % strips
            targets = [orows[j, k, s] for s in range(slots)]
            flags = [omask[j, k, s] * (s + 1) for s in range(slots)]
        for r in range(strips * Q):
            place = jnp.int32(0)
            for s in range(slots):
                place = place + jnp.where(targets[s] == r, flags[s], 0)
            yield r // strips, (r % strips) * tile, place

    def fill(held, across, put):
        for n in range(blocks):
            held[n, 0] = zero
            for s in range(slots):
                block = block_of(n, s)
                held[n, s + 1] = block.T if (n < strips) == across else block
        if across:
            for c in range(1, chunks):
                send_own(c)
        for n in range(blocks):
            for d, low, place in places(n):
                put(d, low, n * tile, held[n, place])

    def put_w(d, low, col, block):
        w[d, low:low + tile, col:col + tile] = block

    def put_wt(d, low, col, block):
        wt[d, col:col + tile, low:low + tile] = block

    fill(tiles, True, put_w)

    def gather_step(idx, c):
        for side, count, src in ((0, q, q - 1 - idx), (1, back, q + 1 + idx)):
            @pl.when(idx < count)
            def _():
                acc[c] += dot(wt[src], inbox[side, idx, c])

    def arrive(idx, c, h):
        for side, count in ((0, q), (1, back)):
            to_right = side == 0

            @pl.when(has_side[side])
            def _():
                z_copy(outbox.at[side, idx, c], to_right, idx, c, h).wait_recv()

            if idx < Q - 1:
                @pl.when((idx < count) & has_side[1 - side])
                def _():
                    z_copy(inbox.at[side, idx, c], to_right, idx + 1, c, h).start()

    def reduce_on(idx, c, h):
        part = slice(h * tile, (h + 1) * tile)
        for side, count in ((0, q), (1, back)):
            to_right = side == 0
            dest = Q - 1 - idx + q if to_right else idx - back
            goes = (idx >= count) & has_side[1 - side]

            @pl.when(goes & has_side[side])
            def _():
                outbox[side, idx + 1, c, part] = (
                    terms[dest, c, part] + inbox[side, idx, c, part].astype(f32)
                ).astype(bf16)

            @pl.when(goes & (count == 0))
            def _():
                outbox[side, idx + 1, c, part] = terms[dest, c, part].astype(bf16)

            @pl.when(goes)
            def _():
                z_copy(outbox.at[side, idx + 1, c], to_right, idx + 1, c, h).start()

    for c in range(chunks):
        for h in range(strips):
            arrive(0, c, h)
        for j in range(partners):
            p_copy(0, j, c).wait_recv()
        for d in range(Q):
            total = dot(w[d, :, :rows], own[c])
            for j in range(partners):
                total += dot(w[d, :, (j + 1) * rows:(j + 2) * rows], pvec[j, c])
            terms[d, c] = total
        for h in range(strips):
            reduce_on(0, c, h)

    fill(tiles_t, False, put_wt)

    for idx in range(1, Q - 1):
        for c in range(chunks):
            for h in range(strips):
                arrive(idx, c, h)
                reduce_on(idx, c, h)
            if idx == 1:
                acc[c] = dot(wt[q], own[c])
                gather_step(0, c)
            gather_step(idx, c)
            last = jnp.maximum(jnp.maximum(q, back) - 1, 1)

            @pl.when(idx == last)
            def _():
                for j in reversed(range(partners)):
                    prod_out[j, c] = acc[c, (j + 1) * rows:(j + 2) * rows].astype(bf16)
                    p_copy(1, j, c).start()

    loads[7].wait()
    for c in range(chunks):
        cols = slice(c * width, (c + 1) * width)
        total = acc[c, :rows] + terms[q, c]
        for j in range(partners):
            p_copy(1, j, c).wait_recv()
            total += prod_in[j, c].astype(f32)
        out[:, cols] = 2.0 / cheb_half * (total - cheb_center * vec[:, cols]) - prev[:, cols]
        for h in range(strips):
            part = slice(h * tile, (h + 1) * tile)
            arrive(Q - 1, c, h)
            for side in range(2):
                @pl.when(has_side[side])
                def _():
                    out[part, cols] += 2.0 / cheb_half * inbox[side, Q - 1, c, part].astype(f32)

    for c in range(chunks):
        for kind in range(2):
            for j in range(partners):
                p_copy(kind, j, c).wait_send()
        for idx in range(Q):
            for h in range(strips):
                for side in range(2):
                    @pl.when(has_side[1 - side])
                    def _():
                        z_copy(outbox.at[side, idx, c], side == 0, idx, c, h).wait_send()


def on_device(vectors, previous, diag_tiles, diag_cols, diag_mask, off_tiles, off_rows, off_mask):
    tile = diag_tiles.shape[-1]
    strips, slots = diag_tiles.shape[:2]
    rows, vec_width = vectors.shape
    quarters = lax.axis_size("qtr")
    levels = lax.axis_size("grp").bit_length() - 1
    bit_list = (0, levels // 2, levels - 1)
    width = vec_width // chunks
    blocks = strips * (1 + partners)
    whole = blocks * tile
    hbm = pl.BlockSpec(memory_space=pltpu.HBM)
    dma = pltpu.SemaphoreType.DMA
    macs = 2 * whole * quarters * rows * vec_width
    return pl.pallas_call(
        functools.partial(kernel, quarters, bit_list),
        out_shape=jax.ShapeDtypeStruct((rows, vec_width), f32),
        in_specs=[hbm] * 8,
        out_specs=pl.BlockSpec(memory_space=pltpu.VMEM),
        scratch_shapes=[
            pltpu.SMEM(diag_cols.shape, jnp.int32),
            pltpu.SMEM(diag_mask.shape, jnp.int32),
            pltpu.SMEM(off_rows.shape, jnp.int32),
            pltpu.SMEM(off_mask.shape, jnp.int32),
            pltpu.VMEM((rows, vec_width), f32),
            pltpu.VMEM((rows, vec_width), f32),
            pltpu.VMEM(diag_tiles.shape, bf16),
            pltpu.VMEM(off_tiles.shape, bf16),
            pltpu.VMEM((blocks, slots + 1, tile, tile), bf16),
            pltpu.VMEM((blocks, slots + 1, tile, tile), bf16),
            pltpu.VMEM((quarters, rows, whole), bf16),
            pltpu.VMEM((quarters, whole, rows), bf16),
            pltpu.VMEM((chunks, rows, width), bf16),
            pltpu.VMEM((partners, chunks, rows, width), bf16),
            pltpu.VMEM((partners, chunks, rows, width), bf16),
            pltpu.VMEM((partners, chunks, rows, width), bf16),
            pltpu.VMEM((2, quarters, chunks, rows, width), bf16),
            pltpu.VMEM((2, quarters, chunks, rows, width), bf16),
            pltpu.VMEM((chunks, whole, width), f32),
            pltpu.VMEM((quarters, chunks, rows, width), f32),
            dma((8,)),
            dma((2, quarters, chunks, strips)),
            dma((2, quarters, chunks, strips)),
            dma((2, partners, chunks)),
            dma((2, partners, chunks)),
        ],
        compiler_params=pltpu.CompilerParams(
            collective_id=0, has_side_effects=True, vmem_limit_bytes=64 << 20
        ),
        cost_estimate=pl.CostEstimate(
            flops=2 * macs, bytes_accessed=4 * rows * vec_width * 4, transcendentals=0
        ),
    )(diag_cols, diag_mask, off_rows, off_mask, vectors, previous, diag_tiles, off_tiles)


def solution(mesh):
    in_specs = (
        P(("grp", "qtr"), None),
        P(("grp", "qtr"), None),
        P(("grp", "qtr"), None, None, None),
        P(("grp", "qtr"), None),
        P(("grp", "qtr"), None),
        P(None, ("grp", "qtr"), None, None, None),
        P(None, ("grp", "qtr"), None),
        P(None, ("grp", "qtr"), None),
    )
    out_specs = P(("grp", "qtr"), None)
    return jax.shard_map(
        on_device, mesh=mesh, in_specs=in_specs, out_specs=out_specs, check_vma=False
    )
```
